32 devices in a mesh: ctx: 16 (over z, y, core), head: 2 (over x).
Axes of the slice: x: 2, y: 2, z: 4, core: 2. Of those that a mesh axis runs over, the one named last changes fastest.
Arguments:
- queries: bfloat16 [4096, 2048], P('ctx', 'head'), may hold values from -120 to 120
- keys: bfloat16 [4096, 128], P('ctx'), may hold values from -20 to 20
- values: bfloat16 [4096, 128], P('ctx'), may hold values from -6 to 6
- grad_out: bfloat16 [4096, 2048], P('ctx', 'head'), may hold values from -6 to 6
- doc_of_block: int32 [16], replicated, may hold values from 0 to 3, never falling along the last dimension, each value on 1 to 8 neighbouring positions
- pair_list: int32 [16, 7], P('ctx'), may hold values from 0 to 7, as said below
- knock: int32 [16, 16], P('head'), may hold values 0 or 1
Outputs:
- d_queries: bfloat16 [4096, 2048], P('ctx', 'head')
- d_keys: bfloat16 [4096, 128], P('ctx')
- d_values: bfloat16 [4096, 128], P('ctx')
The draws below stay inside these ranges and needn't reach their ends.
Inputs may be any that keep to these rules, and one draw needn't show every extreme that they name: `pair_list`: row b holds distinct offsets from 1 to 7 in its first entries and 0 in the rest; some row holds all 7 offsets; an offset that reaches before block 0 names no block. `doc_of_block`: never falls along the blocks; each document covers 1 to 8 whole blocks, one exactly 8.
All inputs are finite; a program needn't handle non-finite values. No bound on the sum of `knock` on one device may be relied on, other than what follows from the above.
Results may differ from the reference program's by a relative error of at most 0.01.
Values may be sent and summed in bfloat16 or wider, within the bound.
A program may use at most 128 MiB of HBM per device.

```python
import math
import jax
import jax.numpy as jnp
import numpy as np
from jax import lax

HD = 128
HEADS = 16
Q_DEV = 256
NB = 16
TOKENS = 4096
WIN = 8
DOCS = 4


def query_key_pair(key):
    first, second = jax.random.split(jax.random.fold_in(key, 7), 2)
    base_keys = jnp.clip(jax.random.normal(second, (TOKENS, HD), jnp.float32), -6.0, 6.0)
    base_queries = jnp.clip(jax.random.normal(first, (TOKENS, HEADS * HD), jnp.float32), -6.0, 6.0)
    keys_out = base_keys
    queries_out = base_queries
    return (queries_out, keys_out)


def draw_queries(key, part):
    return query_key_pair(key)[0].astype(jnp.bfloat16)


def draw_keys(key, part):
    return query_key_pair(key)[1].astype(jnp.bfloat16)


def draw_pair_list(key, part):
    first, second, third = jax.random.split(jax.random.fold_in(key, 3), 3)
    spread = WIN - 1
    columns = jnp.arange(spread, dtype=jnp.int32)
    ranks = jax.random.randint(first, (NB, spread), 0, 1 << 20, jnp.int32) * spread + columns[None, :]
    order = jnp.argsort(ranks, axis=1, stable=True).astype(jnp.int32) + 1
    counts = jax.random.randint(second, (NB,), 0, WIN, jnp.int32)
    fullrow = jax.random.randint(third, (), 0, NB, jnp.int32)
    counts = jnp.where(jnp.arange(NB, dtype=jnp.int32) == fullrow, spread, counts)
    return jnp.where(columns[None, :] < counts[:, None], order, 0).astype(jnp.int32)


def set_ends(array, own_key, low, largest):
    extent = array.shape
    spot = [jax.random.randint(jax.random.fold_in(own_key, axis), (), 0, extent[axis]) for axis in range(len(extent))]
    array = array.at[tuple(spot)].set(low)
    longest = extent.index(max(extent))
    spot[longest] = (spot[longest] + 1) % extent[longest]
    return array.at[tuple(spot)].set(largest)


def level_of(own_key, shape, pieces, low, largest):
    gain = 1.0
    for dim, parts in pieces:
        steps = jax.random.uniform(jax.random.fold_in(jax.random.fold_in(own_key, 6), dim), (parts,), jnp.float32, low / len(pieces), largest / len(pieces))
        gain = gain * jnp.repeat(jnp.exp(steps), shape[dim] // parts).reshape((-1,) + (1,) * (len(shape) - 1 - dim))
    return gain


def length_profile(count, total, limit, lean):
    loads = [(1 << 20) // math.isqrt(grade ** lean) + 1 for grade in range(2, count + 1)]
    surplus, given = total - limit - (count - 1), [1] * (count - 1)
    while surplus > 0:
        movable = [i for i in range(count - 1) if given[i] < limit]
        mass, budget = sum([loads[i] for i in movable]), surplus
        for i in movable:
            extra = min(limit - given[i], max(1, budget * loads[i] // mass), surplus)
            given[i] = given[i] + extra
            surplus = surplus - extra
    return np.array([limit] + given)


def uneven_parts(key, number_of, total, most, lean):
    if number_of == 2:
        one = jax.random.randint(key, (), max(1, total - most), min(most, total - 1) + 1)
        return jnp.stack([one, total - one])
    sizes = jnp.asarray(length_profile(number_of, total, most, lean), jnp.int32)
    pairs = (number_of - 1) // 2
    source_of, receiver = sizes[1:1 + 2 * pairs:2], sizes[2:2 + 2 * pairs:2]
    room = jnp.minimum(source_of - 1, most - receiver)
    passed = jax.random.randint(jax.random.fold_in(key, 1), (pairs,), 0, 1 << 20) % (room + 1)
    sizes = sizes.at[1:1 + 2 * pairs:2].set(source_of - passed).at[2:2 + 2 * pairs:2].set(receiver + passed)
    return sizes[jax.random.permutation(jax.random.fold_in(key, 2), number_of)]


def scatter_about(stream_key, shape, scale, reach, cuts=(), kind=jnp.bfloat16):
    level = level_of(stream_key, shape, cuts, -0.22, 0.18) if cuts else 1.0
    entries = jax.random.normal(stream_key, shape, jnp.float32) * scale * level
    return jnp.minimum(jnp.maximum(entries, -reach), reach).astype(kind)


def setup_inputs(seed: int = 0) -> dict:
    arg_keys = jax.random.split(jax.random.key(seed), 8)
    return {
        "queries": draw_queries(jax.random.fold_in(arg_keys[7], 71), 0),
        "keys": draw_keys(jax.random.fold_in(arg_keys[7], 71), 0),
        "values": scatter_about(arg_keys[2], (TOKENS, HD), 1.0, 6.0, ((0, 16),)),
        "grad_out": scatter_about(arg_keys[3], (TOKENS, HEADS * HD), 1.0, 6.0, ((0, 16), (1, 2))),
        "doc_of_block": jnp.searchsorted(jnp.cumsum(uneven_parts(arg_keys[4], DOCS, NB, WIN, 0)), jnp.arange(NB), side="right").astype(jnp.int32),
        "pair_list": draw_pair_list(jax.random.fold_in(arg_keys[7], 71), 0),
        "knock": set_ends((jax.random.randint(arg_keys[6], (HEADS, NB), 0, 4) < 3).astype(jnp.int32), jax.random.fold_in(arg_keys[6], 1), 0, 1),
    }


NEG = -1e30


def reference(queries, keys, values, grad_out, doc_of_block, pair_list, knock):
    scale = HD ** -0.5
    margin = (WIN - 1) * Q_DEV
    span = WIN * Q_DEV
    key_pad = jnp.concatenate([jnp.zeros((margin, HD), jnp.float32), keys.astype(jnp.float32)], axis=0)
    value_pad = jnp.concatenate([jnp.zeros((margin, HD), jnp.float32), values.astype(jnp.float32)], axis=0)
    query_heads = queries.astype(jnp.float32).reshape(TOKENS, HEADS, HD)
    grad_heads = grad_out.astype(jnp.float32).reshape(TOKENS, HEADS, HD)

    def one_block(carry, block):
        key_grads, value_grads = carry
        start = block * Q_DEV
        query_block = lax.dynamic_slice_in_dim(query_heads, start, Q_DEV, 0)
        grad_block = lax.dynamic_slice_in_dim(grad_heads, start, Q_DEV, 0)
        key_window = lax.dynamic_slice_in_dim(key_pad, start, span, 0)
        value_window = lax.dynamic_slice_in_dim(value_pad, start, span, 0)
        position = start - margin + jnp.arange(span, dtype=jnp.int32)
        source = jnp.floor_divide(position, Q_DEV).astype(jnp.int32)
        offset = block - source
        clipped = jnp.clip(source, 0, NB - 1).astype(jnp.int32)
        listed = (offset == 0) | jnp.any(pair_list[block][None, :] == offset[:, None], axis=1)
        same_doc = doc_of_block[clipped] == doc_of_block[block]
        allowed = (position >= 0) & listed & same_doc
        head_keep = (knock[:, clipped] == 1) | (offset == 0)[None, :]
        row_pos = start + jnp.arange(Q_DEV, dtype=jnp.int32)
        causal = position[None, :] <= row_pos[:, None]
        live = allowed[None, None, :] & head_keep[:, None, :] & causal[None, :, :]
        scores = jnp.einsum("ihd,jd->hij", query_block, key_window) * scale
        masked = jnp.where(live, scores, NEG)
        top = jnp.max(masked, axis=2, keepdims=True)
        total = jnp.sum(jnp.exp(masked - top), axis=2, keepdims=True)
        log_total = top + jnp.log(total)
        probs = jnp.exp(masked - log_total)
        grad_probs = jnp.einsum("ihd,jd->hij", grad_block, value_window)
        delta = jnp.sum(probs * grad_probs, axis=2, keepdims=True)
        grad_scores = probs * (grad_probs - delta)
        probs_low = lax.optimization_barrier(probs.astype(jnp.bfloat16)).astype(jnp.float32)
        grad_low = lax.optimization_barrier(grad_scores.astype(jnp.bfloat16)).astype(jnp.float32)
        query_grad = jnp.einsum("hij,jd->ihd", grad_low, key_window) * scale
        key_part = jnp.einsum("hij,ihd->jd", grad_low, query_block) * scale
        value_part = jnp.einsum("hij,ihd->jd", probs_low, grad_block)
        key_grads = lax.dynamic_update_slice_in_dim(
            key_grads, lax.dynamic_slice_in_dim(key_grads, start, span, 0) + key_part, start, 0)
        value_grads = lax.dynamic_update_slice_in_dim(
            value_grads, lax.dynamic_slice_in_dim(value_grads, start, span, 0) + value_part, start, 0)
        return (key_grads, value_grads), query_grad.reshape(Q_DEV, HEADS * HD).astype(jnp.bfloat16)

    zeros = jnp.zeros((margin + TOKENS, HD), jnp.float32)
    (key_grads, value_grads), query_grads = lax.scan(one_block, (zeros, zeros), jnp.arange(NB, dtype=jnp.int32))
    d_queries = query_grads.reshape(TOKENS, HEADS * HD)
    return d_queries, key_grads[margin:].astype(jnp.bfloat16), value_grads[margin:].astype(jnp.bfloat16)
```

```python
import functools
import math

import jax
import jax.numpy as jnp
from jax import lax
from jax.experimental import pallas as pl
from jax.experimental.pallas import tpu as pltpu
from jax.sharding import PartitionSpec as P

NEG = -1e30
BIG = 1e30
MESH = pl.DeviceIdType.MESH
F32 = jnp.float32
BF16 = jnp.bfloat16


def transposed(x):
    return x.astype(F32).T.astype(BF16)


def kernel(
    n, parts, reach, heads, rows, width,
    q, k, v, g, doc, pair, knock,
    dq, dk, dv,
    kv, qt, gt, e_s, dp_s, tops, top, total, weighted, dqt,
    pf, part, rx, red, rc, fin,
    gather_send, gather_recv, pass_send, pass_recv,
    part_send, part_recv, back_send, back_recv, fin_send, fin_recv,
):
    here = lax.axis_index("ctx")
    mine = lax.axis_index("head")
    scale = width ** (-0.5)
    coef = scale * math.log2(math.e)
    share = 2 * rows // parts
    slots = jnp.minimum(here + 1, reach)
    after = jnp.minimum(n - 1 - here, reach - 1)
    my_rows = pl.ds(pl.multiple_of(mine * share, share), share)

    def peer(t):
        return lax.rem(mine + t, parts)

    def rows_of(index):
        return pl.ds(pl.multiple_of(index * share, share), share)

    def gather_copy(d):
        return pltpu.make_async_remote_copy(
            src_ref=kv.at[0, my_rows], dst_ref=kv.at[d, my_rows],
            send_sem=gather_send.at[d], recv_sem=gather_recv.at[d],
            device_id={"ctx": lax.rem(here + d, n)}, device_id_type=MESH)

    def pass_copy(d, t):
        return pltpu.make_async_remote_copy(
            src_ref=kv.at[d, my_rows], dst_ref=kv.at[d, my_rows],
            send_sem=pass_send.at[d, t - 1], recv_sem=pass_recv.at[d, t - 1],
            device_id={"head": peer(t)}, device_id_type=MESH)

    def pass_arrival(d, t):
        theirs = rows_of(lax.rem(mine + parts - t, parts))
        return pltpu.make_async_remote_copy(
            src_ref=kv.at[d, theirs], dst_ref=kv.at[d, theirs],
            send_sem=pass_send.at[d, t - 1], recv_sem=pass_recv.at[d, t - 1],
            device_id={"head": peer(t)}, device_id_type=MESH)

    def part_copy(o, t):
        return pltpu.make_async_remote_copy(
            src_ref=part.at[o, rows_of(peer(t))], dst_ref=rx.at[o, t - 1],
            send_sem=part_send.at[o, t - 1], recv_sem=part_recv.at[o, t - 1],
            device_id={"head": peer(t)}, device_id_type=MESH)

    def back_copy(o):
        return pltpu.make_async_remote_copy(
            src_ref=red.at[o], dst_ref=rc.at[o],
            send_sem=back_send.at[o], recv_sem=back_recv.at[o],
            device_id={"ctx": lax.rem(here + n - o, n)}, device_id_type=MESH)

    def fin_copy(t):
        return pltpu.make_async_remote_copy(
            src_ref=fin.at[my_rows], dst_ref=fin.at[my_rows],
            send_sem=fin_send.at[t - 1], recv_sem=fin_recv.at[t - 1],
            device_id={"head": peer(t)}, device_id_type=MESH)

    def fin_arrival(t):
        theirs = rows_of(lax.rem(mine + parts - t, parts))
        return pltpu.make_async_remote_copy(
            src_ref=fin.at[theirs], dst_ref=fin.at[theirs],
            send_sem=fin_send.at[t - 1], recv_sem=fin_recv.at[t - 1],
            device_id={"head": peer(t)}, device_id_type=MESH)

    barrier = pltpu.get_barrier_semaphore()

    def greet(d, _):
        @pl.when(d <= after)
        def _():
            pl.semaphore_signal(barrier, inc=1, device_id={"ctx": lax.rem(here + d, n)}, device_id_type=MESH)

        @pl.when(d < slots)
        def _():
            pl.semaphore_signal(barrier, inc=1, device_id={"ctx": lax.rem(here + n - d, n)}, device_id_type=MESH)

        return 0

    lax.fori_loop(1, reach, greet, 0)
    for t in range(1, parts):
        pl.semaphore_signal(barrier, inc=1, device_id={"head": peer(t)}, device_id_type=MESH)
    kv[0, 0:rows, :] = k[...]
    kv[0, rows:2 * rows, :] = v[...]
    pl.semaphore_wait(barrier, after + slots - 1 + parts - 1)

    def send_block(d, _):
        gather_copy(d).start()
        return 0

    lax.fori_loop(1, after + 1, send_block, 0)

    for h in range(heads):
        qt[:, h * rows:(h + 1) * rows] = transposed(q[:, h * width:(h + 1) * width])
        gt[:, h * rows:(h + 1) * rows] = transposed(g[:, h * width:(h + 1) * width])
    dqt[...] = jnp.zeros_like(dqt)

    def forward(d):
        gather_copy(d).wait_recv()
        for t in range(1, parts):
            pass_copy(d, t).start()

    def score_slot(o, own):
        keys = kv[o, 0:rows, :]
        values = kv[o, rows:2 * rows, :]
        if own:
            lower = (lax.broadcasted_iota(jnp.int32, (rows, rows), 0)
                     <= lax.broadcasted_iota(jnp.int32, (rows, rows), 1))
        else:
            source = here - o
            listed = jnp.int32(0)
            for j in range(reach - 1):
                listed = listed + (pair[0, j] == o).astype(jnp.int32)
            allowed = jnp.minimum(listed, 1) * (doc[source] == doc[here]).astype(jnp.int32)
        for h in range(heads):
            cols = slice(h * rows, (h + 1) * rows)
            raw = jnp.dot(keys, qt[:, cols], preferred_element_type=F32)
            grad_probs = jnp.dot(values, gt[:, cols], preferred_element_type=F32)
            if own:
                raw = jnp.where(lower, raw, NEG)
                now = jnp.max(raw, axis=0, keepdims=True) * coef
                shifted = jnp.exp2(raw * coef - now)
                total[h:h + 1, :] = jnp.sum(shifted, axis=0, keepdims=True)
                weighted[h:h + 1, :] = jnp.sum(shifted * grad_probs, axis=0, keepdims=True)
            else:
                live = jnp.full((1, rows), allowed * knock[h, source], jnp.int32) == 1
                before = top[h:h + 1, :]
                now = jnp.where(
                    live, jnp.maximum(before, jnp.max(raw, axis=0, keepdims=True) * coef), before)
                factor = jnp.exp2(before - now)
                shifted = jnp.exp2(raw * coef - jnp.where(live, now, BIG))
                total[h:h + 1, :] = total[h:h + 1, :] * factor + jnp.sum(shifted, axis=0, keepdims=True)
                weighted[h:h + 1, :] = (
                    weighted[h:h + 1, :] * factor + jnp.sum(shifted * grad_probs, axis=0, keepdims=True))
            top[h:h + 1, :] = now
            tops[o, h:h + 1, :] = now
            e_s[o, :, cols] = shifted
            dp_s[o, :, cols] = grad_probs

    @pl.when(slots > 1)
    def _():
        forward(1)

    score_slot(0, True)

    def score_step(o, _):
        @pl.when(o + 1 < slots)
        def _():
            forward(o + 1)

        for t in range(1, parts):
            pass_arrival(o, t).wait_recv()
        score_slot(o, False)
        return 0

    lax.fori_loop(1, slots, score_step, 0)
    total[...] = 1.0 / total[...]
    weighted[...] = weighted[...] * total[...]

    def grad_slot(o):
        keys_t = transposed(kv[o, 0:rows, :])
        key_part = jnp.zeros((rows, width), F32)
        value_part = jnp.zeros((rows, width), F32)
        for h in range(heads):
            cols = slice(h * rows, (h + 1) * rows)
            lanes = slice(h * width, (h + 1) * width)
            factor = jnp.exp2(tops[o, h:h + 1, :] - top[h:h + 1, :]) * total[h:h + 1, :]
            probs = e_s[o, :, cols] * factor
            grad_scores = probs * (dp_s[o, :, cols] - weighted[h:h + 1, :])
            probs_low = probs.astype(BF16)
            grad_low = grad_scores.astype(BF16)
            key_part += jnp.dot(grad_low, q[:, lanes], preferred_element_type=F32)
            value_part += jnp.dot(probs_low, g[:, lanes], preferred_element_type=F32)
            dqt[:, cols] += jnp.dot(keys_t, grad_low, preferred_element_type=F32)
        key_part = key_part * scale
        pf[o, 0:rows, :] = key_part
        pf[o, rows:2 * rows, :] = value_part
        part[o, 0:rows, :] = key_part.astype(BF16)
        part[o, rows:2 * rows, :] = value_part.astype(BF16)

    def head_sum(o):
        out = pf[o, my_rows, :]
        for t in range(1, parts):
            part_copy(o, t).wait_recv()
            out = out + rx[o, t - 1].astype(F32)
        return out

    def send_back(o):
        red[o] = head_sum(o).astype(BF16)
        back_copy(o).start()

    def grad_step(i, _):
        o = slots - 1 - i
        grad_slot(o)
        for t in range(1, parts):
            part_copy(o, t).start()

        @pl.when(i > 0)
        def _():
            send_back(o + 1)

        return 0

    lax.fori_loop(0, slots, grad_step, 0)

    for h in range(heads):
        block = dqt[:, h * rows:(h + 1) * rows] * scale
        dq[:, h * width:(h + 1) * width] = block.T.astype(BF16)

    def take(d, out):
        back_copy(d).wait_recv()
        return out + rc[d].astype(F32)

    result = lax.fori_loop(1, after + 1, take, head_sum(0))
    fin[my_rows, :] = result.astype(BF16)
    for t in range(1, parts):
        fin_copy(t).start()
    for t in range(1, parts):
        fin_arrival(t).wait_recv()
    dk[...] = fin[0:rows, :]
    dv[...] = fin[rows:2 * rows, :]

    def sent_blocks(d, _):
        gather_copy(d).wait_send()
        return 0

    lax.fori_loop(1, after + 1, sent_blocks, 0)

    def sent_slots(o, _):
        for t in range(1, parts):
            part_copy(o, t).wait_send()

        @pl.when(o > 0)
        def _():
            back_copy(o).wait_send()
            for t in range(1, parts):
                pass_copy(o, t).wait_send()

        return 0

    lax.fori_loop(0, slots, sent_slots, 0)
    for t in range(1, parts):
        fin_copy(t).wait_send()


def local(n, parts, queries, keys, values, grad_out, doc_of_block, pair_list, knock):
    rows, width = keys.shape
    heads = queries.shape[1] // width
    reach = min(pair_list.shape[1] + 1, n)
    share = 2 * rows // parts
    others = parts - 1
    vmem = pl.BlockSpec(memory_space=pltpu.VMEM)
    smem = pl.BlockSpec(memory_space=pltpu.SMEM)
    dma = pltpu.SemaphoreType.DMA
    tiles = reach * heads * rows * rows
    return pl.pallas_call(
        functools.partial(kernel, n, parts, reach, heads, rows, width),
        out_shape=(
            jax.ShapeDtypeStruct(queries.shape, BF16),
            jax.ShapeDtypeStruct(keys.shape, BF16),
            jax.ShapeDtypeStruct(values.shape, BF16),
        ),
        in_specs=[vmem] * 4 + [smem] * 3,
        out_specs=(vmem,) * 3,
        scratch_shapes=[
            pltpu.VMEM((reach, 2 * rows, width), BF16),
            pltpu.VMEM((width, heads * rows), BF16),
            pltpu.VMEM((width, heads * rows), BF16),
            pltpu.VMEM((reach, rows, heads * rows), F32),
            pltpu.VMEM((reach, rows, heads * rows), F32),
            pltpu.VMEM((reach, heads, rows), F32),
            pltpu.VMEM((heads, rows), F32),
            pltpu.VMEM((heads, rows), F32),
            pltpu.VMEM((heads, rows), F32),
            pltpu.VMEM((width, heads * rows), F32),
            pltpu.VMEM((reach, 2 * rows, width), F32),
            pltpu.VMEM((reach, 2 * rows, width), BF16),
            pltpu.VMEM((reach, others, share, width), BF16),
            pltpu.VMEM((reach, share, width), BF16),
            pltpu.VMEM((reach, share, width), BF16),
            pltpu.VMEM((2 * rows, width), BF16),
            dma((reach,)), dma((reach,)),
            dma((reach, others)), dma((reach, others)),
            dma((reach, others)), dma((reach, others)),
            dma((reach,)), dma((reach,)),
            dma((others,)), dma((others,)),
        ],
        compiler_params=pltpu.CompilerParams(
            collective_id=0, has_side_effects=True, vmem_limit_bytes=56 * 1024 * 1024),
        cost_estimate=pl.CostEstimate(
            flops=10 * tiles * width, bytes_accessed=4 * 2 * rows * heads * width, transcendentals=tiles),
    )(queries, keys, values, grad_out, doc_of_block, pair_list, knock)


def solution(mesh):
    in_specs = (
        P("ctx", "head"),
        P("ctx", None),
        P("ctx", None),
        P("ctx", "head"),
        P(),
        P("ctx", None),
        P("head", None),
    )
    out_specs = (P("ctx", "head"), P("ctx", None), P("ctx", None))
    body = functools.partial(local, mesh.shape["ctx"], mesh.shape["head"])
    return jax.shard_map(body, mesh=mesh, in_specs=in_specs, out_specs=out_specs, check_vma=False)
```

```python
import functools
import math

import jax
import jax.numpy as jnp
from jax import lax
from jax.experimental import pallas as pl
from jax.experimental.pallas import tpu as pltpu
from jax.sharding import PartitionSpec as P

NEG = -1e30
BIG = 1e30
MESH = pl.DeviceIdType.MESH
F32 = jnp.float32
BF16 = jnp.bfloat16


def transposed(x):
    return x.astype(F32).T.astype(BF16)


def kernel(
    n, parts, reach, heads, rows, width,
    q, k, v, g, doc, pair, knock,
    dq, dk, dv,
    kv, qt, gt, e_s, dp_s, tops, top, total, weighted, dqt,
    pf, part, sx, rx, red, rc, fin,
    gather_send, gather_recv, pass_send, pass_recv, twin_send, twin_recv,
    mate_send, mate_recv,
    part_send, part_recv, back_send, back_recv, fin_send, fin_recv,
):
    here = lax.axis_index("ctx")
    mine = lax.axis_index("head")
    scale = width ** (-0.5)
    coef = scale * math.log2(math.e)
    share = 2 * rows // parts
    side = lax.rem(here, 2)
    twin = here + 1 - 2 * side
    last = reach - 1
    evens = tuple(range(2, reach, 2))
    my_rows = pl.ds(pl.multiple_of(mine * share, share), share)

    def peer(t):
        return lax.rem(mine + t, parts)

    def rows_of(index):
        return pl.ds(pl.multiple_of(index * share, share), share)

    def gather_copy(d):
        return pltpu.make_async_remote_copy(
            src_ref=kv.at[0, my_rows], dst_ref=kv.at[d, my_rows],
            send_sem=gather_send.at[d], recv_sem=gather_recv.at[d],
            device_id={"ctx": lax.rem(here + d, n)}, device_id_type=MESH)

    def pass_copy(d, t):
        return pltpu.make_async_remote_copy(
            src_ref=kv.at[d, my_rows], dst_ref=kv.at[d, my_rows],
            send_sem=pass_send.at[d, t - 1], recv_sem=pass_recv.at[d, t - 1],
            device_id={"head": peer(t)}, device_id_type=MESH)

    def pass_arrival(d, t):
        theirs = rows_of(lax.rem(mine + parts - t, parts))
        return pltpu.make_async_remote_copy(
            src_ref=kv.at[d, theirs], dst_ref=kv.at[d, theirs],
            send_sem=pass_send.at[d, t - 1], recv_sem=pass_recv.at[d, t - 1],
            device_id={"head": peer(t)}, device_id_type=MESH)

    def part_copy(o, t):
        return pltpu.make_async_remote_copy(
            src_ref=part.at[o, rows_of(peer(t))], dst_ref=rx.at[o, t - 1],
            send_sem=part_send.at[o, t - 1], recv_sem=part_recv.at[o, t - 1],
            device_id={"head": peer(t)}, device_id_type=MESH)

    def back_copy(o):
        return pltpu.make_async_remote_copy(
            src_ref=red.at[o], dst_ref=rc.at[o],
            send_sem=back_send.at[o], recv_sem=back_recv.at[o],
            device_id={"ctx": lax.rem(here + n - o, n)}, device_id_type=MESH)

    def fin_copy(t):
        return pltpu.make_async_remote_copy(
            src_ref=fin.at[my_rows], dst_ref=fin.at[my_rows],
            send_sem=fin_send.at[t - 1], recv_sem=fin_recv.at[t - 1],
            device_id={"head": peer(t)}, device_id_type=MESH)

    def fin_arrival(t):
        theirs = rows_of(lax.rem(mine + parts - t, parts))
        return pltpu.make_async_remote_copy(
            src_ref=fin.at[theirs], dst_ref=fin.at[theirs],
            send_sem=fin_send.at[t - 1], recv_sem=fin_recv.at[t - 1],
            device_id={"head": peer(t)}, device_id_type=MESH)

    def twin_copy(r):
        return pltpu.make_async_remote_copy(
            src_ref=kv.at[r], dst_ref=kv.at[r + 1 - 2 * side],
            send_sem=twin_send.at[r], recv_sem=twin_recv.at[r + 1 - 2 * side],
            device_id={"ctx": twin}, device_id_type=MESH)

    def twin_arrival(o):
        return pltpu.make_async_remote_copy(
            src_ref=kv.at[o], dst_ref=kv.at[o],
            send_sem=twin_send.at[o], recv_sem=twin_recv.at[o],
            device_id={"ctx": twin}, device_id_type=MESH)

    def mate_copy(o):
        return pltpu.make_async_remote_copy(
            src_ref=part.at[o], dst_ref=sx.at[o + 1 - 2 * side],
            send_sem=mate_send.at[o], recv_sem=mate_recv.at[o + 1 - 2 * side],
            device_id={"ctx": twin}, device_id_type=MESH)

    def mate_arrival(r):
        return pltpu.make_async_remote_copy(
            src_ref=part.at[r], dst_ref=sx.at[r],
            send_sem=mate_send.at[r], recv_sem=mate_recv.at[r],
            device_id={"ctx": twin}, device_id_type=MESH)

    ahead = [(r, here + r < n) for r in evens] + [(last, (here + last < n) & (side == 1))]
    behind = [(r, here >= r) for r in evens] + [(last, (here >= last) & (side == 0))]

    barrier = pltpu.get_barrier_semaphore()
    greeted = jnp.int32(parts)
    for r, there in ahead:
        greeted = greeted + there.astype(jnp.int32)

        @pl.when(there)
        def _():
            pl.semaphore_signal(barrier, inc=1, device_id={"ctx": lax.rem(here + r, n)}, device_id_type=MESH)

    for r, there in behind:
        greeted = greeted + there.astype(jnp.int32)

        @pl.when(there)
        def _():
            pl.semaphore_signal(barrier, inc=1, device_id={"ctx": lax.rem(here + n - r, n)}, device_id_type=MESH)

    pl.semaphore_signal(barrier, inc=1, device_id={"ctx": twin}, device_id_type=MESH)
    for t in range(1, parts):
        pl.semaphore_signal(barrier, inc=1, device_id={"head": peer(t)}, device_id_type=MESH)
    kv[0, 0:rows, :] = k[...]
    kv[0, rows:2 * rows, :] = v[...]
    pl.semaphore_wait(barrier, greeted)

    for r, there in ahead:
        @pl.when(there)
        def _():
            gather_copy(r).start()

    @pl.when(side == 0)
    def _():
        twin_copy(0).start()

    for h in range(heads):
        qt[:, h * rows:(h + 1) * rows] = transposed(q[:, h * width:(h + 1) * width])
        gt[:, h * rows:(h + 1) * rows] = transposed(g[:, h * width:(h + 1) * width])
    dqt[...] = jnp.zeros_like(dqt)

    def forward(r, there):
        @pl.when(there)
        def _():
            gather_copy(r).wait_recv()
            for t in range(1, parts):
                pass_copy(r, t).start()

    def gathered(r):
        for t in range(1, parts):
            pass_arrival(r, t).wait_recv()

    def score_slot(o, own):
        keys = kv[o, 0:rows, :]
        values = kv[o, rows:2 * rows, :]
        if own:
            lower = (lax.broadcasted_iota(jnp.int32, (rows, rows), 0)
                     <= lax.broadcasted_iota(jnp.int32, (rows, rows), 1))
        else:
            source = here - o
            listed = jnp.int32(0)
            for j in range(reach - 1):
                listed = listed + (pair[0, j] == o).astype(jnp.int32)
            allowed = jnp.minimum(listed, 1) * (doc[source] == doc[here]).astype(jnp.int32)
        for h in range(heads):
            cols = slice(h * rows, (h + 1) * rows)
            raw = jnp.dot(keys, qt[:, cols], preferred_element_type=F32)
            grad_probs = jnp.dot(values, gt[:, cols], preferred_element_type=F32)
            if own:
                raw = jnp.where(lower, raw, NEG)
                now = jnp.max(raw, axis=0, keepdims=True) * coef
                shifted = jnp.exp2(raw * coef - now)
                total[h:h + 1, :] = jnp.sum(shifted, axis=0, keepdims=True)
                weighted[h:h + 1, :] = jnp.sum(shifted * grad_probs, axis=0, keepdims=True)
            else:
                live = jnp.full((1, rows), allowed * knock[h, source], jnp.int32) == 1
                before = top[h:h + 1, :]
                now = jnp.where(
                    live, jnp.maximum(before, jnp.max(raw, axis=0, keepdims=True) * coef), before)
                factor = jnp.exp2(before - now)
                shifted = jnp.exp2(raw * coef - jnp.where(live, now, BIG))
                total[h:h + 1, :] = total[h:h + 1, :] * factor + jnp.sum(shifted, axis=0, keepdims=True)
                weighted[h:h + 1, :] = (
                    weighted[h:h + 1, :] * factor + jnp.sum(shifted * grad_probs, axis=0, keepdims=True))
            top[h:h + 1, :] = now
            tops[o, h:h + 1, :] = now
            e_s[o, :, cols] = shifted
            dp_s[o, :, cols] = grad_probs

    def slot_at(t):
        inner = jnp.where(lax.rem(t, 2) == 1, t + 1, jnp.maximum(t - 1, 0))
        return jnp.where((side == 1) | (t == last), t, inner)

    forward(*behind[0])
    score_slot(0, True)

    def score_step(t, _):
        o = slot_at(t)

        @pl.when(lax.rem(t, 2) == 1)
        def _():
            r = t + 1

            @pl.when((r <= here) & (r < reach))
            def _():
                gathered(r)
                twin_copy(r).start()

            for j in range(1, len(behind)):
                @pl.when(t == 2 * j - 1)
                def _():
                    forward(*behind[j])

        @pl.when(o <= here)
        def _():
            @pl.when((lax.rem(o, 2) == 1) & ((side == 1) | (o < last)))
            def _():
                twin_arrival(o).wait_recv()

            @pl.when((side == 0) & (o == last))
            def _():
                gathered(o)

            score_slot(o, False)

        return 0

    lax.fori_loop(1, reach, score_step, 0)
    total[...] = 1.0 / total[...]
    weighted[...] = weighted[...] * total[...]

    def grad_slot(o):
        keys_t = transposed(kv[o, 0:rows, :])
        key_part = jnp.zeros((rows, width), F32)
        value_part = jnp.zeros((rows, width), F32)
        for h in range(heads):
            cols = slice(h * rows, (h + 1) * rows)
            lanes = slice(h * width, (h + 1) * width)
            factor = jnp.exp2(tops[o, h:h + 1, :] - top[h:h + 1, :]) * total[h:h + 1, :]
            probs = e_s[o, :, cols] * factor
            grad_scores = probs * (dp_s[o, :, cols] - weighted[h:h + 1, :])
            probs_low = probs.astype(BF16)
            grad_low = grad_scores.astype(BF16)
            key_part += jnp.dot(grad_low, q[:, lanes], preferred_element_type=F32)
            value_part += jnp.dot(probs_low, g[:, lanes], preferred_element_type=F32)
            dqt[:, cols] += jnp.dot(keys_t, grad_low, preferred_element_type=F32)
        key_part = key_part * scale
        pf[o, 0:rows, :] = key_part
        pf[o, rows:2 * rows, :] = value_part
        part[o, 0:rows, :] = key_part.astype(BF16)
        part[o, rows:2 * rows, :] = value_part.astype(BF16)

    def head_sum(o):
        out = pf[o, my_rows, :]
        for t in range(1, parts):
            part_copy(o, t).wait_recv()
            out = out + rx[o, t - 1].astype(F32)
        return out

    def send_parts(o):
        for t in range(1, parts):
            part_copy(o, t).start()

    def join_twin(r):
        @pl.when((r > 0) | (side == 0))
        def _():
            mate_arrival(r).wait_recv()
            both = pf[r] + sx[r].astype(F32)
            pf[r] = both
            part[r] = both.astype(BF16)

        send_parts(r)

    def send_back(o):
        red[o] = head_sum(o).astype(BF16)
        back_copy(o).start()

    def grad_step(i, _):
        o = slot_at(last - i)

        @pl.when(o <= here)
        def _():
            grad_slot(o)

            @pl.when((lax.rem(o, 2) == 1) & ((side == 1) | (o < last)))
            def _():
                mate_copy(o).start()

            @pl.when((side == 0) & (o == last))
            def _():
                send_parts(o)

        u = i - 1 + side

        @pl.when(lax.rem(u, 2) == 0)
        def _():
            @pl.when((u >= 2) & (reach - u <= here))
            def _():
                join_twin(reach - u)

            @pl.when((u >= 4) & (reach + 2 - u <= here))
            def _():
                send_back(reach + 2 - u)

        @pl.when((side == 0) & (i == 2) & (here >= last))
        def _():
            send_back(jnp.int32(last))

        return 0

    lax.fori_loop(0, reach, grad_step, 0)
    join_twin(0)

    @pl.when(here >= 2)
    def _():
        send_back(2)

    for h in range(heads):
        block = dqt[:, h * rows:(h + 1) * rows] * scale
        dq[:, h * width:(h + 1) * width] = block.T.astype(BF16)

    pf[0, my_rows, :] = head_sum(0)
    for r, there in reversed(ahead):
        @pl.when(there)
        def _():
            back_copy(r).wait_recv()
            pf[0, my_rows, :] += rc[r].astype(F32)

    fin[my_rows, :] = pf[0, my_rows, :].astype(BF16)
    for t in range(1, parts):
        fin_copy(t).start()
    for t in range(1, parts):
        fin_arrival(t).wait_recv()
    dk[...] = fin[0:rows, :]
    dv[...] = fin[rows:2 * rows, :]

    for r, there in ahead:
        @pl.when(there)
        def _():
            gather_copy(r).wait_send()

    for r, there in behind:
        @pl.when(there)
        def _():
            back_copy(r).wait_send()
            for t in range(1, parts):
                pass_copy(r, t).wait_send()
                part_copy(r, t).wait_send()

    for t in range(1, parts):
        part_copy(0, t).wait_send()
        fin_copy(t).wait_send()
    for r in (0,) + evens:
        @pl.when((here >= r) & ((r > 0) | (side == 0)))
        def _():
            twin_copy(r).wait_send()

    for o in range(1, reach, 2):
        @pl.when((o <= here) & ((side == 1) | (o < last)))
        def _():
            mate_copy(o).wait_send()


def finish(*refs):
    count = (len(refs) - 1) // 2
    sems = refs[-1]
    copies = [pltpu.make_async_copy(refs[i], refs[count + i], sems.at[i]) for i in range(count)]
    for copy in copies:
        copy.start()
    for copy in copies:
        copy.wait()


def local(n, parts, queries, keys, values, grad_out, doc_of_block, pair_list, knock):
    rows, width = keys.shape
    heads = queries.shape[1] // width
    reach = min(pair_list.shape[1] + 1, n)
    share = 2 * rows // parts
    others = parts - 1
    vmem = pl.BlockSpec(memory_space=pltpu.VMEM)
    smem = pl.BlockSpec(memory_space=pltpu.SMEM)
    dma = pltpu.SemaphoreType.DMA
    tiles = reach * heads * rows * rows
    results = pl.pallas_call(
        functools.partial(kernel, n, parts, reach, heads, rows, width),
        out_shape=(
            jax.ShapeDtypeStruct(queries.shape, BF16),
            jax.ShapeDtypeStruct(keys.shape, BF16),
            jax.ShapeDtypeStruct(values.shape, BF16),
        ),
        in_specs=[vmem] * 4 + [smem] * 3,
        out_specs=(vmem,) * 3,
        scratch_shapes=[
            pltpu.VMEM((reach, 2 * rows, width), BF16),
            pltpu.VMEM((width, heads * rows), BF16),
            pltpu.VMEM((width, heads * rows), BF16),
            pltpu.VMEM((reach, rows, heads * rows), F32),
            pltpu.VMEM((reach, rows, heads * rows), F32),
            pltpu.VMEM((reach, heads, rows), F32),
            pltpu.VMEM((heads, rows), F32),
            pltpu.VMEM((heads, rows), F32),
            pltpu.VMEM((heads, rows), F32),
            pltpu.VMEM((width, heads * rows), F32),
            pltpu.VMEM((reach, 2 * rows, width), F32),
            pltpu.VMEM((reach, 2 * rows, width), BF16),
            pltpu.VMEM((reach, 2 * rows, width), BF16),
            pltpu.VMEM((reach, others, share, width), BF16),
            pltpu.VMEM((reach, share, width), BF16),
            pltpu.VMEM((reach, share, width), BF16),
            pltpu.VMEM((2 * rows, width), BF16),
            dma((reach,)), dma((reach,)),
            dma((reach, others)), dma((reach, others)),
            dma((reach,)), dma((reach,)),
            dma((reach,)), dma((reach,)),
            dma((reach, others)), dma((reach, others)),
            dma((reach,)), dma((reach,)),
            dma((others,)), dma((others,)),
        ],
        compiler_params=pltpu.CompilerParams(
            collective_id=0, has_side_effects=True, vmem_limit_bytes=56 * 1024 * 1024),
        cost_estimate=pl.CostEstimate(
            flops=10 * tiles * width, bytes_accessed=4 * 2 * rows * heads * width, transcendentals=tiles),
    )(queries, keys, values, grad_out, doc_of_block, pair_list, knock)
    anywhere = pl.BlockSpec(memory_space=pl.ANY)
    return pl.pallas_call(
        finish,
        out_shape=tuple(jax.ShapeDtypeStruct(x.shape, x.dtype) for x in results),
        in_specs=[anywhere] * 3,
        out_specs=(anywhere,) * 3,
        scratch_shapes=[dma((3,))],
        compiler_params=pltpu.CompilerParams(vmem_limit_bytes=56 * 1024 * 1024),
    )(*results)


def solution(mesh):
    in_specs = (
        P("ctx", "head"),
        P("ctx", None),
        P("ctx", None),
        P("ctx", "head"),
        P(),
        P("ctx", None),
        P("head", None),
    )
    out_specs = (P("ctx", "head"), P("ctx", None), P("ctx", None))
    body = functools.partial(local, mesh.shape["ctx"], mesh.shape["head"])
    return jax.shard_map(body, mesh=mesh, in_specs=in_specs, out_specs=out_specs, check_vma=False)
```

```python
import functools
import math

import jax
import jax.numpy as jnp
from jax import lax
from jax.experimental import pallas as pl
from jax.experimental.pallas import tpu as pltpu
from jax.sharding import PartitionSpec as P

NEG = -1e30
BIG = 1e30
MESH = pl.DeviceIdType.MESH
F32 = jnp.float32
BF16 = jnp.bfloat16


def transposed(x):
    return x.astype(F32).T.astype(BF16)


def kernel(
    n, parts, reach, heads, rows, width,
    q, k, v, g, doc, pair, knock,
    dq, dk, dv,
    kv, qt, gt, qs, gs, p_low, g_low, e_s, dp_s, tops, top, total, weighted, dqt,
    pf, part, sx, rx, red, rc, fin,
    gather_send, gather_recv, pass_send, pass_recv, twin_send, twin_recv,
    mate_send, mate_recv,
    part_send, part_recv, back_send, back_recv, fin_send, fin_recv,
):
    here = lax.axis_index("ctx")
    mine = lax.axis_index("head")
    scale = width ** (-0.5)
    coef = scale * math.log2(math.e)
    share = 2 * rows // parts
    side = lax.rem(here, 2)
    twin = here + 1 - 2 * side
    last = reach - 1
    evens = tuple(range(2, reach, 2))
    my_rows = pl.ds(pl.multiple_of(mine * share, share), share)

    def peer(t):
        return lax.rem(mine + t, parts)

    def rows_of(index):
        return pl.ds(pl.multiple_of(index * share, share), share)

    def gather_copy(d):
        return pltpu.make_async_remote_copy(
            src_ref=kv.at[0, my_rows], dst_ref=kv.at[d, my_rows],
            send_sem=gather_send.at[d], recv_sem=gather_recv.at[d],
            device_id={"ctx": lax.rem(here + d, n)}, device_id_type=MESH)

    def pass_copy(d, t):
        return pltpu.make_async_remote_copy(
            src_ref=kv.at[d, my_rows], dst_ref=kv.at[d, my_rows],
            send_sem=pass_send.at[d, t - 1], recv_sem=pass_recv.at[d, t - 1],
            device_id={"head": peer(t)}, device_id_type=MESH)

    def pass_arrival(d, t):
        theirs = rows_of(lax.rem(mine + parts - t, parts))
        return pltpu.make_async_remote_copy(
            src_ref=kv.at[d, theirs], dst_ref=kv.at[d, theirs],
            send_sem=pass_send.at[d, t - 1], recv_sem=pass_recv.at[d, t - 1],
            device_id={"head": peer(t)}, device_id_type=MESH)

    def part_copy(o, t):
        return pltpu.make_async_remote_copy(
            src_ref=part.at[o, rows_of(peer(t))], dst_ref=rx.at[o, t - 1],
            send_sem=part_send.at[o, t - 1], recv_sem=part_recv.at[o, t - 1],
            device_id={"head": peer(t)}, device_id_type=MESH)

    def back_copy(o):
        return pltpu.make_async_remote_copy(
            src_ref=red.at[o], dst_ref=rc.at[o],
            send_sem=back_send.at[o], recv_sem=back_recv.at[o],
            device_id={"ctx": lax.rem(here + n - o, n)}, device_id_type=MESH)

    def fin_copy(t):
        return pltpu.make_async_remote_copy(
            src_ref=fin.at[my_rows], dst_ref=fin.at[my_rows],
            send_sem=fin_send.at[t - 1], recv_sem=fin_recv.at[t - 1],
            device_id={"head": peer(t)}, device_id_type=MESH)

    def fin_arrival(t):
        theirs = rows_of(lax.rem(mine + parts - t, parts))
        return pltpu.make_async_remote_copy(
            src_ref=fin.at[theirs], dst_ref=fin.at[theirs],
            send_sem=fin_send.at[t - 1], recv_sem=fin_recv.at[t - 1],
            device_id={"head": peer(t)}, device_id_type=MESH)

    def twin_copy(r):
        return pltpu.make_async_remote_copy(
            src_ref=kv.at[r], dst_ref=kv.at[r + 1 - 2 * side],
            send_sem=twin_send.at[r], recv_sem=twin_recv.at[r + 1 - 2 * side],
            device_id={"ctx": twin}, device_id_type=MESH)

    def twin_arrival(o):
        return pltpu.make_async_remote_copy(
            src_ref=kv.at[o], dst_ref=kv.at[o],
            send_sem=twin_send.at[o], recv_sem=twin_recv.at[o],
            device_id={"ctx": twin}, device_id_type=MESH)

    def mate_copy(o):
        return pltpu.make_async_remote_copy(
            src_ref=part.at[o], dst_ref=sx.at[o + 1 - 2 * side],
            send_sem=mate_send.at[o], recv_sem=mate_recv.at[o + 1 - 2 * side],
            device_id={"ctx": twin}, device_id_type=MESH)

    def mate_arrival(r):
        return pltpu.make_async_remote_copy(
            src_ref=part.at[r], dst_ref=sx.at[r],
            send_sem=mate_send.at[r], recv_sem=mate_recv.at[r],
            device_id={"ctx": twin}, device_id_type=MESH)

    ahead = [(r, here + r < n) for r in evens] + [(last, (here + last < n) & (side == 1))]
    behind = [(r, here >= r) for r in evens] + [(last, (here >= last) & (side == 0))]

    barrier = pltpu.get_barrier_semaphore()
    greeted = jnp.int32(parts)
    for r, there in ahead:
        greeted = greeted + there.astype(jnp.int32)

        @pl.when(there)
        def _():
            pl.semaphore_signal(barrier, inc=1, device_id={"ctx": lax.rem(here + r, n)}, device_id_type=MESH)

    for r, there in behind:
        greeted = greeted + there.astype(jnp.int32)

        @pl.when(there)
        def _():
            pl.semaphore_signal(barrier, inc=1, device_id={"ctx": lax.rem(here + n - r, n)}, device_id_type=MESH)

    pl.semaphore_signal(barrier, inc=1, device_id={"ctx": twin}, device_id_type=MESH)
    for t in range(1, parts):
        pl.semaphore_signal(barrier, inc=1, device_id={"head": peer(t)}, device_id_type=MESH)
    kv[0, 0:rows, :] = k[...]
    kv[0, rows:2 * rows, :] = v[...]
    pl.semaphore_wait(barrier, greeted)

    for r, there in ahead:
        @pl.when(there)
        def _():
            gather_copy(r).start()

    @pl.when(side == 0)
    def _():
        twin_copy(0).start()

    for h in range(heads):
        qt[:, h * rows:(h + 1) * rows] = transposed(q[:, h * width:(h + 1) * width])
        gt[:, h * rows:(h + 1) * rows] = transposed(g[:, h * width:(h + 1) * width])
        qs[h * rows:(h + 1) * rows, :] = q[:, h * width:(h + 1) * width]
        gs[h * rows:(h + 1) * rows, :] = g[:, h * width:(h + 1) * width]
    dqt[...] = jnp.zeros_like(dqt)

    def forward(r, there):
        @pl.when(there)
        def _():
            gather_copy(r).wait_recv()
            for t in range(1, parts):
                pass_copy(r, t).start()

    def gathered(r):
        for t in range(1, parts):
            pass_arrival(r, t).wait_recv()

    def score_slot(o, own):
        keys = kv[o, 0:rows, :]
        values = kv[o, rows:2 * rows, :]
        if own:
            lower = (lax.broadcasted_iota(jnp.int32, (rows, rows), 0)
                     <= lax.broadcasted_iota(jnp.int32, (rows, rows), 1))
        else:
            source = here - o
            listed = jnp.int32(0)
            for j in range(reach - 1):
                listed = listed + (pair[0, j] == o).astype(jnp.int32)
            allowed = jnp.minimum(listed, 1) * (doc[source] == doc[here]).astype(jnp.int32)
        for h in range(heads):
            cols = slice(h * rows, (h + 1) * rows)
            raw = jnp.dot(keys, qt[:, cols], preferred_element_type=F32)
            grad_probs = jnp.dot(values, gt[:, cols], preferred_element_type=F32)
            if own:
                raw = jnp.where(lower, raw, NEG)
                now = jnp.max(raw, axis=0, keepdims=True) * coef
                shifted = jnp.exp2(raw * coef - now)
                total[h:h + 1, :] = jnp.sum(shifted, axis=0, keepdims=True)
                weighted[h:h + 1, :] = jnp.sum(shifted * grad_probs, axis=0, keepdims=True)
            else:
                live = jnp.full((1, rows), allowed * knock[h, source], jnp.int32) == 1
                before = top[h:h + 1, :]
                now = jnp.where(
                    live, jnp.maximum(before, jnp.max(raw, axis=0, keepdims=True) * coef), before)
                factor = jnp.exp2(before - now)
                shifted = jnp.exp2(raw * coef - jnp.where(live, now, BIG))
                total[h:h + 1, :] = total[h:h + 1, :] * factor + jnp.sum(shifted, axis=0, keepdims=True)
                weighted[h:h + 1, :] = (
                    weighted[h:h + 1, :] * factor + jnp.sum(shifted * grad_probs, axis=0, keepdims=True))
            top[h:h + 1, :] = now
            tops[o, h:h + 1, :] = now
            e_s[o, :, cols] = shifted
            dp_s[o, :, cols] = grad_probs

    def slot_at(t):
        inner = jnp.where(lax.rem(t, 2) == 1, t + 1, jnp.maximum(t - 1, 0))
        return jnp.where((side == 1) | (t == last), t, inner)

    forward(*behind[0])
    score_slot(0, True)

    def score_step(t, _):
        o = slot_at(t)

        @pl.when(lax.rem(t, 2) == 1)
        def _():
            r = t + 1

            @pl.when((r <= here) & (r < reach))
            def _():
                gathered(r)
                twin_copy(r).start()

            for j in range(1, len(behind)):
                @pl.when(t == 2 * j - 1)
                def _():
                    forward(*behind[j])

        @pl.when(o <= here)
        def _():
            @pl.when((lax.rem(o, 2) == 1) & ((side == 1) | (o < last)))
            def _():
                twin_arrival(o).wait_recv()

            @pl.when((side == 0) & (o == last))
            def _():
                gathered(o)

            score_slot(o, False)

        return 0

    lax.fori_loop(1, reach, score_step, 0)
    total[...] = 1.0 / total[...]
    weighted[...] = weighted[...] * total[...]

    def grad_slot(o):
        keys_t = transposed(kv[o, 0:rows, :])
        for h in range(heads):
            cols = slice(h * rows, (h + 1) * rows)
            factor = jnp.exp2(tops[o, h:h + 1, :] - top[h:h + 1, :]) * total[h:h + 1, :]
            probs = e_s[o, :, cols] * factor
            grad_scores = probs * (dp_s[o, :, cols] - weighted[h:h + 1, :])
            p_low[:, cols] = probs.astype(BF16)
            g_low[:, cols] = grad_scores.astype(BF16)
        key_part = jnp.dot(g_low[...], qs[...], preferred_element_type=F32) * scale
        value_part = jnp.dot(p_low[...], gs[...], preferred_element_type=F32)
        dqt[...] += jnp.dot(keys_t, g_low[...], preferred_element_type=F32)
        pf[o, 0:rows, :] = key_part
        pf[o, rows:2 * rows, :] = value_part
        part[o, 0:rows, :] = key_part.astype(BF16)
        part[o, rows:2 * rows, :] = value_part.astype(BF16)

    def head_sum(o):
        out = pf[o, my_rows, :]
        for t in range(1, parts):
            part_copy(o, t).wait_recv()
            out = out + rx[o, t - 1].astype(F32)
        return out

    def send_parts(o):
        for t in range(1, parts):
            part_copy(o, t).start()

    def join_twin(r):
        @pl.when((r > 0) | (side == 0))
        def _():
            mate_arrival(r).wait_recv()
            both = pf[r] + sx[r].astype(F32)
            pf[r] = both
            part[r] = both.astype(BF16)

        send_parts(r)

    def send_back(o):
        red[o] = head_sum(o).astype(BF16)
        back_copy(o).start()

    def grad_step(i, _):
        o = slot_at(last - i)

        @pl.when(o <= here)
        def _():
            grad_slot(o)

            @pl.when((lax.rem(o, 2) == 1) & ((side == 1) | (o < last)))
            def _():
                mate_copy(o).start()

            @pl.when((side == 0) & (o == last))
            def _():
                send_parts(o)

        @pl.when(lax.rem(i, 2) == 0)
        def _():
            @pl.when((i >= 2) & (reach - i <= here))
            def _():
                join_twin(reach - i)

            @pl.when((i >= 4) & (reach + 2 - i <= here))
            def _():
                send_back(reach + 2 - i)

        @pl.when((side == 0) & (i == 2) & (here >= last))
        def _():
            send_back(jnp.int32(last))

        return 0

    lax.fori_loop(0, reach, grad_step, 0)

    @pl.when(here >= 2)
    def _():
        send_back(2)

    join_twin(0)

    for h in range(heads):
        block = dqt[:, h * rows:(h + 1) * rows] * scale
        dq[:, h * width:(h + 1) * width] = block.T.astype(BF16)

    pf[0, my_rows, :] = head_sum(0)
    for r, there in reversed(ahead):
        @pl.when(there)
        def _():
            back_copy(r).wait_recv()
            pf[0, my_rows, :] += rc[r].astype(F32)

    fin[my_rows, :] = pf[0, my_rows, :].astype(BF16)
    for t in range(1, parts):
        fin_copy(t).start()
    for t in range(1, parts):
        fin_arrival(t).wait_recv()
    dk[...] = fin[0:rows, :]
    dv[...] = fin[rows:2 * rows, :]

    for r, there in ahead:
        @pl.when(there)
        def _():
            gather_copy(r).wait_send()

    for r, there in behind:
        @pl.when(there)
        def _():
            back_copy(r).wait_send()
            for t in range(1, parts):
                pass_copy(r, t).wait_send()
                part_copy(r, t).wait_send()

    for t in range(1, parts):
        part_copy(0, t).wait_send()
        fin_copy(t).wait_send()
    for r in (0,) + evens:
        @pl.when((here >= r) & ((r > 0) | (side == 0)))
        def _():
            twin_copy(r).wait_send()

    for o in range(1, reach, 2):
        @pl.when((o <= here) & ((side == 1) | (o < last)))
        def _():
            mate_copy(o).wait_send()


def finish(*refs):
    count = len(refs) // 2
    for i in range(count):
        refs[count + i][...] = refs[i][...]


def local(n, parts, queries, keys, values, grad_out, doc_of_block, pair_list, knock):
    rows, width = keys.shape
    heads = queries.shape[1] // width
    reach = min(pair_list.shape[1] + 1, n)
    share = 2 * rows // parts
    others = parts - 1
    vmem = pl.BlockSpec(memory_space=pltpu.VMEM)
    smem = pl.BlockSpec(memory_space=pltpu.SMEM)
    dma = pltpu.SemaphoreType.DMA
    tiles = reach * heads * rows * rows
    results = pl.pallas_call(
        functools.partial(kernel, n, parts, reach, heads, rows, width),
        out_shape=(
            jax.ShapeDtypeStruct(queries.shape, BF16),
            jax.ShapeDtypeStruct(keys.shape, BF16),
            jax.ShapeDtypeStruct(values.shape, BF16),
        ),
        in_specs=[vmem] * 4 + [smem] * 3,
        out_specs=(vmem,) * 3,
        scratch_shapes=[
            pltpu.VMEM((reach, 2 * rows, width), BF16),
            pltpu.VMEM((width, heads * rows), BF16),
            pltpu.VMEM((width, heads * rows), BF16),
            pltpu.VMEM((heads * rows, width), BF16),
            pltpu.VMEM((heads * rows, width), BF16),
            pltpu.VMEM((rows, heads * rows), BF16),
            pltpu.VMEM((rows, heads * rows), BF16),
            pltpu.VMEM((reach, rows, heads * rows), F32),
            pltpu.VMEM((reach, rows, heads * rows), F32),
            pltpu.VMEM((reach, heads, rows), F32),
            pltpu.VMEM((heads, rows), F32),
            pltpu.VMEM((heads, rows), F32),
            pltpu.VMEM((heads, rows), F32),
            pltpu.VMEM((width, heads * rows), F32),
            pltpu.VMEM((reach, 2 * rows, width), F32),
            pltpu.VMEM((reach, 2 * rows, width), BF16),
            pltpu.VMEM((reach, 2 * rows, width), BF16),
            pltpu.VMEM((reach, others, share, width), BF16),
            pltpu.VMEM((reach, share, width), BF16),
            pltpu.VMEM((reach, share, width), BF16),
            pltpu.VMEM((2 * rows, width), BF16),
            dma((reach,)), dma((reach,)),
            dma((reach, others)), dma((reach, others)),
            dma((reach,)), dma((reach,)),
            dma((reach,)), dma((reach,)),
            dma((reach, others)), dma((reach, others)),
            dma((reach,)), dma((reach,)),
            dma((others,)), dma((others,)),
        ],
        compiler_params=pltpu.CompilerParams(
            collective_id=0, has_side_effects=True, vmem_limit_bytes=56 * 1024 * 1024),
        cost_estimate=pl.CostEstimate(
            flops=10 * tiles * width, bytes_accessed=4 * 2 * rows * heads * width, transcendentals=tiles),
    )(queries, keys, values, grad_out, doc_of_block, pair_list, knock)
    return pl.pallas_call(
        finish,
        out_shape=tuple(jax.ShapeDtypeStruct(x.shape, x.dtype) for x in results),
        in_specs=[vmem] * 3,
        out_specs=(vmem,) * 3,
    )(*results)


def solution(mesh):
    in_specs = (
        P("ctx", "head"),
        P("ctx", None),
        P("ctx", None),
        P("ctx", "head"),
        P(),
        P("ctx", None),
        P("head", None),
    )
    out_specs = (P("ctx", "head"), P("ctx", None), P("ctx", None))
    body = functools.partial(local, mesh.shape["ctx"], mesh.shape["head"])
    return jax.shard_map(body, mesh=mesh, in_specs=in_specs, out_specs=out_specs, check_vma=False)
```

```python
import functools
import math

import jax
import jax.numpy as jnp
from jax import lax
from jax.experimental import pallas as pl
from jax.experimental.pallas import tpu as pltpu
from jax.sharding import PartitionSpec as P

NEG = -1e30
BIG = 1e30
MESH = pl.DeviceIdType.MESH
F32 = jnp.float32
BF16 = jnp.bfloat16


def transposed(x):
    return x.astype(F32).T.astype(BF16)


def kernel(
    n, parts, reach, heads, rows, width,
    q, k, v, g, doc, pair, knock,
    dq, dk, dv,
    kv, qt, gt, qs, gs, p_low, g_low, e_s, dp_s, tops, top, total, weighted, dqt,
    pf, part, sx, rx, red, rc, fin,
    gather_send, gather_recv, pass_send, pass_recv, twin_send, twin_recv,
    mate_send, mate_recv,
    part_send, part_recv, back_send, back_recv, fin_send, fin_recv,
):
    here = lax.axis_index("ctx")
    mine = lax.axis_index("head")
    scale = width ** (-0.5)
    coef = scale * math.log2(math.e)
    share = 2 * rows // parts
    side = lax.rem(here, 2)
    twin = here + 1 - 2 * side
    last = reach - 1
    evens = tuple(range(2, reach, 2))
    my_rows = pl.ds(pl.multiple_of(mine * share, share), share)

    def peer(t):
        return lax.rem(mine + t, parts)

    def rows_of(index):
        return pl.ds(pl.multiple_of(index * share, share), share)

    def gather_copy(d):
        return pltpu.make_async_remote_copy(
            src_ref=kv.at[0, my_rows], dst_ref=kv.at[d, my_rows],
            send_sem=gather_send.at[d], recv_sem=gather_recv.at[d],
            device_id={"ctx": lax.rem(here + d, n)}, device_id_type=MESH)

    def pass_copy(d, t):
        return pltpu.make_async_remote_copy(
            src_ref=kv.at[d, my_rows], dst_ref=kv.at[d, my_rows],
            send_sem=pass_send.at[d, t - 1], recv_sem=pass_recv.at[d, t - 1],
            device_id={"head": peer(t)}, device_id_type=MESH)

    def pass_arrival(d, t):
        theirs = rows_of(lax.rem(mine + parts - t, parts))
        return pltpu.make_async_remote_copy(
            src_ref=kv.at[d, theirs], dst_ref=kv.at[d, theirs],
            send_sem=pass_send.at[d, t - 1], recv_sem=pass_recv.at[d, t - 1],
            device_id={"head": peer(t)}, device_id_type=MESH)

    def part_copy(o, t):
        return pltpu.make_async_remote_copy(
            src_ref=part.at[o, rows_of(peer(t))], dst_ref=rx.at[o, t - 1],
            send_sem=part_send.at[o, t - 1], recv_sem=part_recv.at[o, t - 1],
            device_id={"head": peer(t)}, device_id_type=MESH)

    def back_copy(o):
        return pltpu.make_async_remote_copy(
            src_ref=red.at[o], dst_ref=rc.at[o],
            send_sem=back_send.at[o], recv_sem=back_recv.at[o],
            device_id={"ctx": lax.rem(here + n - o, n)}, device_id_type=MESH)

    def fin_copy(t):
        return pltpu.make_async_remote_copy(
            src_ref=fin.at[my_rows], dst_ref=fin.at[my_rows],
            send_sem=fin_send.at[t - 1], recv_sem=fin_recv.at[t - 1],
            device_id={"head": peer(t)}, device_id_type=MESH)

    def fin_arrival(t):
        theirs = rows_of(lax.rem(mine + parts - t, parts))
        return pltpu.make_async_remote_copy(
            src_ref=fin.at[theirs], dst_ref=fin.at[theirs],
            send_sem=fin_send.at[t - 1], recv_sem=fin_recv.at[t - 1],
            device_id={"head": peer(t)}, device_id_type=MESH)

    def twin_copy(r):
        return pltpu.make_async_remote_copy(
            src_ref=kv.at[r], dst_ref=kv.at[r + 1 - 2 * side],
            send_sem=twin_send.at[r], recv_sem=twin_recv.at[r + 1 - 2 * side],
            device_id={"ctx": twin}, device_id_type=MESH)

    def twin_arrival(o):
        return pltpu.make_async_remote_copy(
            src_ref=kv.at[o], dst_ref=kv.at[o],
            send_sem=twin_send.at[o], recv_sem=twin_recv.at[o],
            device_id={"ctx": twin}, device_id_type=MESH)

    def mate_copy(o):
        return pltpu.make_async_remote_copy(
            src_ref=part.at[o], dst_ref=sx.at[o + 1 - 2 * side],
            send_sem=mate_send.at[o], recv_sem=mate_recv.at[o + 1 - 2 * side],
            device_id={"ctx": twin}, device_id_type=MESH)

    def mate_arrival(r):
        return pltpu.make_async_remote_copy(
            src_ref=part.at[r], dst_ref=sx.at[r],
            send_sem=mate_send.at[r], recv_sem=mate_recv.at[r],
            device_id={"ctx": twin}, device_id_type=MESH)

    ahead = [(r, here + r < n) for r in evens] + [(last, (here + last < n) & (side == 1))]
    behind = [(r, here >= r) for r in evens] + [(last, (here >= last) & (side == 0))]

    barrier = pltpu.get_barrier_semaphore()
    greeted = jnp.int32(parts)
    for r, there in ahead:
        greeted = greeted + there.astype(jnp.int32)

        @pl.when(there)
        def _():
            pl.semaphore_signal(barrier, inc=1, device_id={"ctx": lax.rem(here + r, n)}, device_id_type=MESH)

    for r, there in behind:
        greeted = greeted + there.astype(jnp.int32)

        @pl.when(there)
        def _():
            pl.semaphore_signal(barrier, inc=1, device_id={"ctx": lax.rem(here + n - r, n)}, device_id_type=MESH)

    pl.semaphore_signal(barrier, inc=1, device_id={"ctx": twin}, device_id_type=MESH)
    for t in range(1, parts):
        pl.semaphore_signal(barrier, inc=1, device_id={"head": peer(t)}, device_id_type=MESH)
    kv[0, 0:rows, :] = k[...]
    kv[0, rows:2 * rows, :] = v[...]
    pl.semaphore_wait(barrier, greeted)

    for r, there in ahead:
        @pl.when(there)
        def _():
            gather_copy(r).start()

    @pl.when(side == 0)
    def _():
        twin_copy(0).start()

    for h in range(heads):
        qt[:, h * rows:(h + 1) * rows] = transposed(q[:, h * width:(h + 1) * width])
        gt[:, h * rows:(h + 1) * rows] = transposed(g[:, h * width:(h + 1) * width])
        qs[h * rows:(h + 1) * rows, :] = q[:, h * width:(h + 1) * width]
        gs[h * rows:(h + 1) * rows, :] = g[:, h * width:(h + 1) * width]
    dqt[...] = jnp.zeros_like(dqt)

    def forward(r, there):
        @pl.when(there)
        def _():
            gather_copy(r).wait_recv()
            for t in range(1, parts):
                pass_copy(r, t).start()

    def gathered(r):
        for t in range(1, parts):
            pass_arrival(r, t).wait_recv()

    def score_slot(o, own):
        keys = kv[o, 0:rows, :]
        values = kv[o, rows:2 * rows, :]
        if own:
            lower = (lax.broadcasted_iota(jnp.int32, (rows, rows), 0)
                     <= lax.broadcasted_iota(jnp.int32, (rows, rows), 1))
        else:
            source = here - o
            listed = jnp.int32(0)
            for j in range(reach - 1):
                listed = listed + (pair[0, j] == o).astype(jnp.int32)
            allowed = jnp.minimum(listed, 1) * (doc[source] == doc[here]).astype(jnp.int32)

        def products(h):
            cols = slice(h * rows, (h + 1) * rows)
            raw = jnp.dot(keys, qt[:, cols], preferred_element_type=F32)
            if own:
                raw = jnp.where(lower, raw, NEG)
            e_s[o, :, cols] = raw
            dp_s[o, :, cols] = jnp.dot(values, gt[:, cols], preferred_element_type=F32)
            return jnp.max(raw, axis=0, keepdims=True) * coef

        highest = [products(0)]
        for h in range(heads):
            if h + 1 < heads:
                highest.append(products(h + 1))
            cols = slice(h * rows, (h + 1) * rows)
            raw = e_s[o, :, cols]
            grad_probs = dp_s[o, :, cols]
            if own:
                now = highest[h]
                shifted = jnp.exp2(raw * coef - now)
                total[h:h + 1, :] = jnp.sum(shifted, axis=0, keepdims=True)
                weighted[h:h + 1, :] = jnp.sum(shifted * grad_probs, axis=0, keepdims=True)
            else:
                live = jnp.full((1, rows), allowed * knock[h, source], jnp.int32) == 1
                before = top[h:h + 1, :]
                now = jnp.where(live, jnp.maximum(before, highest[h]), before)
                factor = jnp.exp2(before - now)
                shifted = jnp.exp2(raw * coef - jnp.where(live, now, BIG))
                total[h:h + 1, :] = total[h:h + 1, :] * factor + jnp.sum(shifted, axis=0, keepdims=True)
                weighted[h:h + 1, :] = (
                    weighted[h:h + 1, :] * factor + jnp.sum(shifted * grad_probs, axis=0, keepdims=True))
            top[h:h + 1, :] = now
            tops[o, h:h + 1, :] = now
            e_s[o, :, cols] = shifted

    def slot_at(t):
        inner = jnp.where(lax.rem(t, 2) == 1, t + 1, jnp.maximum(t - 1, 0))
        return jnp.where((side == 1) | (t == last), t, inner)

    forward(*behind[0])
    score_slot(0, True)

    def score_step(t, _):
        o = slot_at(t)

        @pl.when(lax.rem(t, 2) == 1)
        def _():
            r = t + 1

            @pl.when((r <= here) & (r < reach))
            def _():
                gathered(r)
                twin_copy(r).start()

            for j in range(1, len(behind)):
                @pl.when(t == 2 * j - 1)
                def _():
                    forward(*behind[j])

        @pl.when(o <= here)
        def _():
            @pl.when((lax.rem(o, 2) == 1) & ((side == 1) | (o < last)))
            def _():
                twin_arrival(o).wait_recv()

            @pl.when((side == 0) & (o == last))
            def _():
                gathered(o)

            score_slot(o, False)

        return 0

    lax.fori_loop(1, reach, score_step, 0)
    total[...] = 1.0 / total[...]
    weighted[...] = weighted[...] * total[...]

    def grad_slot(o):
        keys_t = transposed(kv[o, 0:rows, :])
        for h in range(heads):
            cols = slice(h * rows, (h + 1) * rows)
            factor = jnp.exp2(tops[o, h:h + 1, :] - top[h:h + 1, :]) * total[h:h + 1, :]
            probs = e_s[o, :, cols] * factor
            grad_scores = probs * (dp_s[o, :, cols] - weighted[h:h + 1, :])
            p_low[:, cols] = probs.astype(BF16)
            g_low[:, cols] = grad_scores.astype(BF16)
        key_part = jnp.dot(g_low[...], qs[...], preferred_element_type=F32) * scale
        value_part = jnp.dot(p_low[...], gs[...], preferred_element_type=F32)
        dqt[...] += jnp.dot(keys_t, g_low[...], preferred_element_type=F32)
        pf[o, 0:rows, :] = key_part
        pf[o, rows:2 * rows, :] = value_part
        part[o, 0:rows, :] = key_part.astype(BF16)
        part[o, rows:2 * rows, :] = value_part.astype(BF16)

    def head_sum(o):
        out = pf[o, my_rows, :]
        for t in range(1, parts):
            part_copy(o, t).wait_recv()
            out = out + rx[o, t - 1].astype(F32)
        return out

    def send_parts(o):
        for t in range(1, parts):
            part_copy(o, t).start()

    def join_twin(r):
        @pl.when((r > 0) | (side == 0))
        def _():
            mate_arrival(r).wait_recv()
            both = pf[r] + sx[r].astype(F32)
            pf[r] = both
            part[r] = both.astype(BF16)

        send_parts(r)

    def send_back(o):
        red[o] = head_sum(o).astype(BF16)
        back_copy(o).start()

    def grad_step(i, _):
        o = slot_at(last - i)

        @pl.when(o <= here)
        def _():
            grad_slot(o)

            @pl.when((lax.rem(o, 2) == 1) & ((side == 1) | (o < last)))
            def _():
                mate_copy(o).start()

            @pl.when((side == 0) & (o == last))
            def _():
                send_parts(o)

        @pl.when(lax.rem(i, 2) == 0)
        def _():
            @pl.when((i >= 2) & (reach - i <= here))
            def _():
                join_twin(reach - i)

            @pl.when((i >= 4) & (reach + 2 - i <= here))
            def _():
                send_back(reach + 2 - i)

        @pl.when((side == 0) & (i == 2) & (here >= last))
        def _():
            send_back(jnp.int32(last))

        return 0

    lax.fori_loop(0, reach, grad_step, 0)

    @pl.when(here >= 2)
    def _():
        send_back(2)

    join_twin(0)

    for h in range(heads):
        block = dqt[:, h * rows:(h + 1) * rows] * scale
        dq[:, h * width:(h + 1) * width] = block.T.astype(BF16)

    pf[0, my_rows, :] = head_sum(0)
    for r, there in reversed(ahead):
        @pl.when(there)
        def _():
            back_copy(r).wait_recv()
            pf[0, my_rows, :] += rc[r].astype(F32)

    fin[my_rows, :] = pf[0, my_rows, :].astype(BF16)
    for t in range(1, parts):
        fin_copy(t).start()
    for t in range(1, parts):
        fin_arrival(t).wait_recv()
    dk[...] = fin[0:rows, :]
    dv[...] = fin[rows:2 * rows, :]

    for r, there in ahead:
        @pl.when(there)
        def _():
            gather_copy(r).wait_send()

    for r, there in behind:
        @pl.when(there)
        def _():
            back_copy(r).wait_send()
            for t in range(1, parts):
                pass_copy(r, t).wait_send()
                part_copy(r, t).wait_send()

    for t in range(1, parts):
        part_copy(0, t).wait_send()
        fin_copy(t).wait_send()
    for r in (0,) + evens:
        @pl.when((here >= r) & ((r > 0) | (side == 0)))
        def _():
            twin_copy(r).wait_send()

    for o in range(1, reach, 2):
        @pl.when((o <= here) & ((side == 1) | (o < last)))
        def _():
            mate_copy(o).wait_send()


def finish(*refs):
    count = len(refs) // 2
    for i in range(count):
        refs[count + i][...] = refs[i][...]


def local(n, parts, queries, keys, values, grad_out, doc_of_block, pair_list, knock):
    rows, width = keys.shape
    heads = queries.shape[1] // width
    reach = min(pair_list.shape[1] + 1, n)
    share = 2 * rows // parts
    others = parts - 1
    vmem = pl.BlockSpec(memory_space=pltpu.VMEM)
    smem = pl.BlockSpec(memory_space=pltpu.SMEM)
    dma = pltpu.SemaphoreType.DMA
    tiles = reach * heads * rows * rows
    results = pl.pallas_call(
        functools.partial(kernel, n, parts, reach, heads, rows, width),
        out_shape=(
            jax.ShapeDtypeStruct(queries.shape, BF16),
            jax.ShapeDtypeStruct(keys.shape, BF16),
            jax.ShapeDtypeStruct(values.shape, BF16),
        ),
        in_specs=[vmem] * 4 + [smem] * 3,
        out_specs=(vmem,) * 3,
        scratch_shapes=[
            pltpu.VMEM((reach, 2 * rows, width), BF16),
            pltpu.VMEM((width, heads * rows), BF16),
            pltpu.VMEM((width, heads * rows), BF16),
            pltpu.VMEM((heads * rows, width), BF16),
            pltpu.VMEM((heads * rows, width), BF16),
            pltpu.VMEM((rows, heads * rows), BF16),
            pltpu.VMEM((rows, heads * rows), BF16),
            pltpu.VMEM((reach, rows, heads * rows), F32),
            pltpu.VMEM((reach, rows, heads * rows), F32),
            pltpu.VMEM((reach, heads, rows), F32),
            pltpu.VMEM((heads, rows), F32),
            pltpu.VMEM((heads, rows), F32),
            pltpu.VMEM((heads, rows), F32),
            pltpu.VMEM((width, heads * rows), F32),
            pltpu.VMEM((reach, 2 * rows, width), F32),
            pltpu.VMEM((reach, 2 * rows, width), BF16),
            pltpu.VMEM((reach, 2 * rows, width), BF16),
            pltpu.VMEM((reach, others, share, width), BF16),
            pltpu.VMEM((reach, share, width), BF16),
            pltpu.VMEM((reach, share, width), BF16),
            pltpu.VMEM((2 * rows, width), BF16),
            dma((reach,)), dma((reach,)),
            dma((reach, others)), dma((reach, others)),
            dma((reach,)), dma((reach,)),
            dma((reach,)), dma((reach,)),
            dma((reach, others)), dma((reach, others)),
            dma((reach,)), dma((reach,)),
            dma((others,)), dma((others,)),
        ],
        compiler_params=pltpu.CompilerParams(
            collective_id=0, has_side_effects=True, vmem_limit_bytes=56 * 1024 * 1024),
        cost_estimate=pl.CostEstimate(
            flops=10 * tiles * width, bytes_accessed=4 * 2 * rows * heads * width, transcendentals=tiles),
    )(queries, keys, values, grad_out, doc_of_block, pair_list, knock)
    return pl.pallas_call(
        finish,
        out_shape=tuple(jax.ShapeDtypeStruct(x.shape, x.dtype) for x in results),
        in_specs=[vmem] * 3,
        out_specs=(vmem,) * 3,
    )(*results)


def solution(mesh):
    in_specs = (
        P("ctx", "head"),
        P("ctx", None),
        P("ctx", None),
        P("ctx", "head"),
        P(),
        P("ctx", None),
        P("head", None),
    )
    out_specs = (P("ctx", "head"), P("ctx", None), P("ctx", None))
    body = functools.partial(local, mesh.shape["ctx"], mesh.shape["head"])
    return jax.shard_map(body, mesh=mesh, in_specs=in_specs, out_specs=out_specs, check_vma=False)
```

```python
import functools
import math

import jax
import jax.numpy as jnp
from jax import lax
from jax.experimental import pallas as pl
from jax.experimental.pallas import tpu as pltpu
from jax.sharding import PartitionSpec as P

NEG = -1e30
BIG = 1e30
MESH = pl.DeviceIdType.MESH
F32 = jnp.float32
BF16 = jnp.bfloat16


def transposed(x):
    return x.astype(F32).T.astype(BF16)


def kernel(
    n, parts, reach, heads, rows, width,
    q_hbm, k, v, g_hbm, doc, pair, knock,
    dq_hbm, dk, dv,
    q, g, dq, local_sem,
    kv, qt, gt, qs, gs, p_low, g_low, e_s, dp_s, tops, top, total, weighted, dqt,
    pf, part, sx, rx, red, rc, fin,
    gather_send, gather_recv, pass_send, pass_recv, twin_send, twin_recv,
    mate_send, mate_recv,
    part_send, part_recv, back_send, back_recv, fin_send, fin_recv,
):
    here = lax.axis_index("ctx")
    mine = lax.axis_index("head")
    scale = width ** (-0.5)
    coef = scale * math.log2(math.e)
    share = 2 * rows // parts
    side = lax.rem(here, 2)
    twin = here + 1 - 2 * side
    last = reach - 1
    evens = tuple(range(2, reach, 2))
    my_rows = pl.ds(pl.multiple_of(mine * share, share), share)

    def peer(t):
        return lax.rem(mine + t, parts)

    def rows_of(index):
        return pl.ds(pl.multiple_of(index * share, share), share)

    def gather_copy(d):
        return pltpu.make_async_remote_copy(
            src_ref=kv.at[0, my_rows], dst_ref=kv.at[d, my_rows],
            send_sem=gather_send.at[d], recv_sem=gather_recv.at[d],
            device_id={"ctx": lax.rem(here + d, n)}, device_id_type=MESH)

    def pass_copy(d, t):
        return pltpu.make_async_remote_copy(
            src_ref=kv.at[d, my_rows], dst_ref=kv.at[d, my_rows],
            send_sem=pass_send.at[d, t - 1], recv_sem=pass_recv.at[d, t - 1],
            device_id={"head": peer(t)}, device_id_type=MESH)

    def pass_arrival(d, t):
        theirs = rows_of(lax.rem(mine + parts - t, parts))
        return pltpu.make_async_remote_copy(
            src_ref=kv.at[d, theirs], dst_ref=kv.at[d, theirs],
            send_sem=pass_send.at[d, t - 1], recv_sem=pass_recv.at[d, t - 1],
            device_id={"head": peer(t)}, device_id_type=MESH)

    def part_copy(o, t):
        return pltpu.make_async_remote_copy(
            src_ref=part.at[o, rows_of(peer(t))], dst_ref=rx.at[o, t - 1],
            send_sem=part_send.at[o, t - 1], recv_sem=part_recv.at[o, t - 1],
            device_id={"head": peer(t)}, device_id_type=MESH)

    def back_copy(o):
        return pltpu.make_async_remote_copy(
            src_ref=red.at[o], dst_ref=rc.at[o],
            send_sem=back_send.at[o], recv_sem=back_recv.at[o],
            device_id={"ctx": lax.rem(here + n - o, n)}, device_id_type=MESH)

    def fin_copy(t):
        return pltpu.make_async_remote_copy(
            src_ref=fin.at[my_rows], dst_ref=fin.at[my_rows],
            send_sem=fin_send.at[t - 1], recv_sem=fin_recv.at[t - 1],
            device_id={"head": peer(t)}, device_id_type=MESH)

    def fin_arrival(t):
        theirs = rows_of(lax.rem(mine + parts - t, parts))
        return pltpu.make_async_remote_copy(
            src_ref=fin.at[theirs], dst_ref=fin.at[theirs],
            send_sem=fin_send.at[t - 1], recv_sem=fin_recv.at[t - 1],
            device_id={"head": peer(t)}, device_id_type=MESH)

    def twin_copy(r):
        return pltpu.make_async_remote_copy(
            src_ref=kv.at[r], dst_ref=kv.at[r + 1 - 2 * side],
            send_sem=twin_send.at[r], recv_sem=twin_recv.at[r + 1 - 2 * side],
            device_id={"ctx": twin}, device_id_type=MESH)

    def twin_arrival(o):
        return pltpu.make_async_remote_copy(
            src_ref=kv.at[o], dst_ref=kv.at[o],
            send_sem=twin_send.at[o], recv_sem=twin_recv.at[o],
            device_id={"ctx": twin}, device_id_type=MESH)

    def mate_copy(o):
        return pltpu.make_async_remote_copy(
            src_ref=part.at[o], dst_ref=sx.at[o + 1 - 2 * side],
            send_sem=mate_send.at[o], recv_sem=mate_recv.at[o + 1 - 2 * side],
            device_id={"ctx": twin}, device_id_type=MESH)

    def mate_arrival(r):
        return pltpu.make_async_remote_copy(
            src_ref=part.at[r], dst_ref=sx.at[r],
            send_sem=mate_send.at[r], recv_sem=mate_recv.at[r],
            device_id={"ctx": twin}, device_id_type=MESH)

    ahead = [(r, here + r < n) for r in evens] + [(last, (here + last < n) & (side == 1))]
    behind = [(r, here >= r) for r in evens] + [(last, (here >= last) & (side == 0))]

    load_q = pltpu.make_async_copy(q_hbm, q, local_sem.at[0])
    load_g = pltpu.make_async_copy(g_hbm, g, local_sem.at[1])
    store_dq = pltpu.make_async_copy(dq, dq_hbm, local_sem.at[2])
    load_q.start()
    load_g.start()

    barrier = pltpu.get_barrier_semaphore()
    greeted = jnp.int32(parts)
    for r, there in ahead:
        greeted = greeted + there.astype(jnp.int32)

        @pl.when(there)
        def _():
            pl.semaphore_signal(barrier, inc=1, device_id={"ctx": lax.rem(here + r, n)}, device_id_type=MESH)

    for r, there in behind:
        greeted = greeted + there.astype(jnp.int32)

        @pl.when(there)
        def _():
            pl.semaphore_signal(barrier, inc=1, device_id={"ctx": lax.rem(here + n - r, n)}, device_id_type=MESH)

    pl.semaphore_signal(barrier, inc=1, device_id={"ctx": twin}, device_id_type=MESH)
    for t in range(1, parts):
        pl.semaphore_signal(barrier, inc=1, device_id={"head": peer(t)}, device_id_type=MESH)
    kv[0, 0:rows, :] = k[...]
    kv[0, rows:2 * rows, :] = v[...]
    pl.semaphore_wait(barrier, greeted)

    for r, there in ahead:
        @pl.when(there)
        def _():
            gather_copy(r).start()

    @pl.when(side == 0)
    def _():
        twin_copy(0).start()

    load_q.wait()
    load_g.wait()
    for h in range(heads):
        qt[:, h * rows:(h + 1) * rows] = transposed(q[:, h * width:(h + 1) * width])
        gt[:, h * rows:(h + 1) * rows] = transposed(g[:, h * width:(h + 1) * width])
        qs[h * rows:(h + 1) * rows, :] = q[:, h * width:(h + 1) * width]
        gs[h * rows:(h + 1) * rows, :] = g[:, h * width:(h + 1) * width]
    dqt[...] = jnp.zeros_like(dqt)

    def forward(r, there):
        @pl.when(there)
        def _():
            gather_copy(r).wait_recv()
            for t in range(1, parts):
                pass_copy(r, t).start()

    def gathered(r):
        for t in range(1, parts):
            pass_arrival(r, t).wait_recv()

    def score_slot(o, own):
        keys = kv[o, 0:rows, :]
        values = kv[o, rows:2 * rows, :]
        if own:
            lower = (lax.broadcasted_iota(jnp.int32, (rows, rows), 0)
                     <= lax.broadcasted_iota(jnp.int32, (rows, rows), 1))
        else:
            source = here - o
            listed = jnp.int32(0)
            for j in range(reach - 1):
                listed = listed + (pair[0, j] == o).astype(jnp.int32)
            allowed = jnp.minimum(listed, 1) * (doc[source] == doc[here]).astype(jnp.int32)

        def products(h):
            cols = slice(h * rows, (h + 1) * rows)
            raw = jnp.dot(keys, qt[:, cols], preferred_element_type=F32)
            if own:
                raw = jnp.where(lower, raw, NEG)
            e_s[o, :, cols] = raw
            dp_s[o, :, cols] = jnp.dot(values, gt[:, cols], preferred_element_type=F32)
            return jnp.max(raw, axis=0, keepdims=True) * coef

        highest = [products(0)]
        for h in range(heads):
            if h + 1 < heads:
                highest.append(products(h + 1))
            cols = slice(h * rows, (h + 1) * rows)
            raw = e_s[o, :, cols]
            grad_probs = dp_s[o, :, cols]
            if own:
                now = highest[h]
                shifted = jnp.exp2(raw * coef - now)
                total[h:h + 1, :] = jnp.sum(shifted, axis=0, keepdims=True)
                weighted[h:h + 1, :] = jnp.sum(shifted * grad_probs, axis=0, keepdims=True)
            else:
                live = jnp.full((1, rows), allowed * knock[h, source], jnp.int32) == 1
                before = top[h:h + 1, :]
                now = jnp.where(live, jnp.maximum(before, highest[h]), before)
                factor = jnp.exp2(before - now)
                shifted = jnp.exp2(raw * coef - jnp.where(live, now, BIG))
                total[h:h + 1, :] = total[h:h + 1, :] * factor + jnp.sum(shifted, axis=0, keepdims=True)
                weighted[h:h + 1, :] = (
                    weighted[h:h + 1, :] * factor + jnp.sum(shifted * grad_probs, axis=0, keepdims=True))
            top[h:h + 1, :] = now
            tops[o, h:h + 1, :] = now
            e_s[o, :, cols] = shifted

    def slot_at(t):
        inner = jnp.where(lax.rem(t, 2) == 1, t + 1, jnp.maximum(t - 1, 0))
        return jnp.where((side == 1) | (t == last), t, inner)

    forward(*behind[0])
    score_slot(0, True)

    def score_step(t, _):
        o = slot_at(t)

        @pl.when(lax.rem(t, 2) == 1)
        def _():
            r = t + 1

            @pl.when((r <= here) & (r < reach))
            def _():
                gathered(r)
                twin_copy(r).start()

            for j in range(1, len(behind)):
                @pl.when(t == 2 * j - 1)
                def _():
                    forward(*behind[j])

        @pl.when(o <= here)
        def _():
            @pl.when((lax.rem(o, 2) == 1) & ((side == 1) | (o < last)))
            def _():
                twin_arrival(o).wait_recv()

            @pl.when((side == 0) & (o == last))
            def _():
                gathered(o)

            score_slot(o, False)

        return 0

    lax.fori_loop(1, reach, score_step, 0)
    total[...] = 1.0 / total[...]
    weighted[...] = weighted[...] * total[...]

    def grad_slot(o):
        keys_t = transposed(kv[o, 0:rows, :])
        for h in range(heads):
            cols = slice(h * rows, (h + 1) * rows)
            factor = jnp.exp2(tops[o, h:h + 1, :] - top[h:h + 1, :]) * total[h:h + 1, :]
            probs = e_s[o, :, cols] * factor
            grad_scores = probs * (dp_s[o, :, cols] - weighted[h:h + 1, :])
            p_low[:, cols] = probs.astype(BF16)
            g_low[:, cols] = grad_scores.astype(BF16)
        key_part = jnp.dot(g_low[...], qs[...], preferred_element_type=F32) * scale
        value_part = jnp.dot(p_low[...], gs[...], preferred_element_type=F32)
        dqt[...] += jnp.dot(keys_t, g_low[...], preferred_element_type=F32)
        pf[o, 0:rows, :] = key_part
        pf[o, rows:2 * rows, :] = value_part
        part[o, 0:rows, :] = key_part.astype(BF16)
        part[o, rows:2 * rows, :] = value_part.astype(BF16)

    def head_sum(o):
        out = pf[o, my_rows, :]
        for t in range(1, parts):
            part_copy(o, t).wait_recv()
            out = out + rx[o, t - 1].astype(F32)
        return out

    def send_parts(o):
        for t in range(1, parts):
            part_copy(o, t).start()

    def join_twin(r):
        @pl.when((r > 0) | (side == 0))
        def _():
            mate_arrival(r).wait_recv()
            both = pf[r] + sx[r].astype(F32)
            pf[r] = both
            part[r] = both.astype(BF16)

        send_parts(r)

    def send_back(o):
        red[o] = head_sum(o).astype(BF16)
        back_copy(o).start()

    def grad_step(i, _):
        o = slot_at(last - i)

        @pl.when(o <= here)
        def _():
            grad_slot(o)

            @pl.when((lax.rem(o, 2) == 1) & ((side == 1) | (o < last)))
            def _():
                mate_copy(o).start()

            @pl.when((side == 0) & (o == last))
            def _():
                send_parts(o)

        @pl.when(lax.rem(i, 2) == 0)
        def _():
            @pl.when((i >= 2) & (reach - i <= here))
            def _():
                join_twin(reach - i)

            @pl.when((i >= 4) & (reach + 2 - i <= here))
            def _():
                send_back(reach + 2 - i)

        @pl.when((side == 0) & (i == 2) & (here >= last))
        def _():
            send_back(jnp.int32(last))

        return 0

    lax.fori_loop(0, reach, grad_step, 0)

    @pl.when(here >= 2)
    def _():
        send_back(2)

    join_twin(0)

    for h in range(heads):
        block = dqt[:, h * rows:(h + 1) * rows] * scale
        dq[:, h * width:(h + 1) * width] = block.T.astype(BF16)

    store_dq.start()
    pf[0, my_rows, :] = head_sum(0)
    for r, there in reversed(ahead):
        @pl.when(there)
        def _():
            back_copy(r).wait_recv()
            pf[0, my_rows, :] += rc[r].astype(F32)

    fin[my_rows, :] = pf[0, my_rows, :].astype(BF16)
    for t in range(1, parts):
        fin_copy(t).start()
    for t in range(1, parts):
        fin_arrival(t).wait_recv()
    dk[...] = fin[0:rows, :]
    dv[...] = fin[rows:2 * rows, :]

    store_dq.wait()
    for r, there in ahead:
        @pl.when(there)
        def _():
            gather_copy(r).wait_send()

    for r, there in behind:
        @pl.when(there)
        def _():
            back_copy(r).wait_send()
            for t in range(1, parts):
                pass_copy(r, t).wait_send()
                part_copy(r, t).wait_send()

    for t in range(1, parts):
        part_copy(0, t).wait_send()
        fin_copy(t).wait_send()
    for r in (0,) + evens:
        @pl.when((here >= r) & ((r > 0) | (side == 0)))
        def _():
            twin_copy(r).wait_send()

    for o in range(1, reach, 2):
        @pl.when((o <= here) & ((side == 1) | (o < last)))
        def _():
            mate_copy(o).wait_send()


def finish(*refs):
    count = len(refs) // 2
    for i in range(count):
        refs[count + i][...] = refs[i][...]


def local(n, parts, queries, keys, values, grad_out, doc_of_block, pair_list, knock):
    rows, width = keys.shape
    heads = queries.shape[1] // width
    reach = min(pair_list.shape[1] + 1, n)
    share = 2 * rows // parts
    others = parts - 1
    vmem = pl.BlockSpec(memory_space=pltpu.VMEM)
    anywhere = pl.BlockSpec(memory_space=pl.ANY)
    smem = pl.BlockSpec(memory_space=pltpu.SMEM)
    dma = pltpu.SemaphoreType.DMA
    tiles = reach * heads * rows * rows
    results = pl.pallas_call(
        functools.partial(kernel, n, parts, reach, heads, rows, width),
        out_shape=(
            jax.ShapeDtypeStruct(queries.shape, BF16),
            jax.ShapeDtypeStruct(keys.shape, BF16),
            jax.ShapeDtypeStruct(values.shape, BF16),
        ),
        in_specs=[anywhere, vmem, vmem, anywhere] + [smem] * 3,
        out_specs=(anywhere, vmem, vmem),
        scratch_shapes=[
            pltpu.VMEM(queries.shape, BF16),
            pltpu.VMEM(queries.shape, BF16),
            pltpu.VMEM(queries.shape, BF16),
            dma((3,)),
            pltpu.VMEM((reach, 2 * rows, width), BF16),
            pltpu.VMEM((width, heads * rows), BF16),
            pltpu.VMEM((width, heads * rows), BF16),
            pltpu.VMEM((heads * rows, width), BF16),
            pltpu.VMEM((heads * rows, width), BF16),
            pltpu.VMEM((rows, heads * rows), BF16),
            pltpu.VMEM((rows, heads * rows), BF16),
            pltpu.VMEM((reach, rows, heads * rows), F32),
            pltpu.VMEM((reach, rows, heads * rows), F32),
            pltpu.VMEM((reach, heads, rows), F32),
            pltpu.VMEM((heads, rows), F32),
            pltpu.VMEM((heads, rows), F32),
            pltpu.VMEM((heads, rows), F32),
            pltpu.VMEM((width, heads * rows), F32),
            pltpu.VMEM((reach, 2 * rows, width), F32),
            pltpu.VMEM((reach, 2 * rows, width), BF16),
            pltpu.VMEM((reach, 2 * rows, width), BF16),
            pltpu.VMEM((reach, others, share, width), BF16),
            pltpu.VMEM((reach, share, width), BF16),
            pltpu.VMEM((reach, share, width), BF16),
            pltpu.VMEM((2 * rows, width), BF16),
            dma((reach,)), dma((reach,)),
            dma((reach, others)), dma((reach, others)),
            dma((reach,)), dma((reach,)),
            dma((reach,)), dma((reach,)),
            dma((reach, others)), dma((reach, others)),
            dma((reach,)), dma((reach,)),
            dma((others,)), dma((others,)),
        ],
        compiler_params=pltpu.CompilerParams(
            collective_id=0, has_side_effects=True, vmem_limit_bytes=56 * 1024 * 1024),
        cost_estimate=pl.CostEstimate(
            flops=10 * tiles * width, bytes_accessed=4 * 2 * rows * heads * width, transcendentals=tiles),
    )(queries, keys, values, grad_out, doc_of_block, pair_list, knock)
    return pl.pallas_call(
        finish,
        out_shape=tuple(jax.ShapeDtypeStruct(x.shape, x.dtype) for x in results),
        in_specs=[vmem] * 3,
        out_specs=(vmem,) * 3,
    )(*results)


def solution(mesh):
    in_specs = (
        P("ctx", "head"),
        P("ctx", None),
        P("ctx", None),
        P("ctx", "head"),
        P(),
        P("ctx", None),
        P("head", None),
    )
    out_specs = (P("ctx", "head"), P("ctx", None), P("ctx", None))
    body = functools.partial(local, mesh.shape["ctx"], mesh.shape["head"])
    return jax.shard_map(body, mesh=mesh, in_specs=in_specs, out_specs=out_specs, check_vma=False)
```
